32 devices in a mesh: mp: 4 (over z), ffn: 8 (over y, x, core).
Axes of the slice: x: 2, y: 2, z: 4, core: 2. Of those that a mesh axis runs over, the one named last changes fastest.
Arguments:
- tokens: bfloat16 [1024, 8192], P('ffn', 'mp'), may hold values from -6 to 6
- gate_weight: bfloat16 [8192, 28672], P('mp', 'ffn'), may hold values from -0.0625 to 0.0625
- up_weight: bfloat16 [8192, 28672], P('mp', 'ffn'), may hold values from -0.0625 to 0.0625
- down_weight: bfloat16 [28672, 8192], P('ffn', 'mp'), may hold values from -0.03125 to 0.03125
Outputs:
- mixed: bfloat16 [1024, 8192], P('ffn', 'mp')
The draws below stay inside these ranges and needn't reach their ends.
All inputs are finite; a program needn't handle non-finite values.
Results may differ from the reference program's by a relative error of at most 0.03.
Values may be sent and summed in bfloat16 or wider, within the bound.
A program may use at most 128 MiB of HBM per device.

```python
import jax
import jax.numpy as jnp
from jax import lax

D = 8192
FF = 28672
TOKENS = 1024
N_MP = 4


def level_of(rng, dims, split, least, top_value):
    loudness, own = 1.0, jax.random.fold_in(rng, 6)
    for position, parts in split:
        steps = jnp.exp(jax.random.uniform(jax.random.fold_in(own, position), (parts,), jnp.float32, least / len(split), top_value / len(split)))
        loudness = loudness * jnp.repeat(steps, dims[position] // parts).reshape([-1 if axis == position else 1 for axis in range(len(dims))])
    return loudness


def normal_values(rng, shape, scale, bound, split=(), held_as=jnp.bfloat16):
    gain = level_of(rng, shape, split, -0.22, 0.18) if split else 1.0
    entries = jax.random.normal(rng, shape, jnp.float32) * scale * gain
    return jnp.minimum(jnp.maximum(entries, -bound), bound).astype(held_as)


def setup_inputs(seed: int = 0) -> dict:
    splits = jax.random.split(jax.random.key(seed), 5)
    tokens = normal_values(splits[0], (TOKENS, D), 1.0, 6.0, ((0, 8), (1, 4)))
    gate_weight = normal_values(splits[1], (D, FF), D ** -0.5, 0.0625, ((0, 4), (1, 8)))
    up_weight = normal_values(splits[2], (D, FF), D ** -0.5, 0.0625, ((0, 4), (1, 8)))
    down_weight = normal_values(splits[3], (FF, D), FF ** -0.5, 0.03125, ((0, 8), (1, 4)))
    return {"tokens": tokens, "gate_weight": gate_weight, "up_weight": up_weight, "down_weight": down_weight}


def reference(tokens, gate_weight, up_weight, down_weight):
    width = D // N_MP
    gate = jnp.zeros((TOKENS, FF), jnp.float32)
    up = jnp.zeros((TOKENS, FF), jnp.float32)
    for block in range(N_MP):
        lower = block * width
        block_tokens = tokens[:, lower:lower + width]
        gate_part = jnp.dot(block_tokens, gate_weight[lower:lower + width], preferred_element_type=jnp.float32).astype(jnp.bfloat16)
        up_part = jnp.dot(block_tokens, up_weight[lower:lower + width], preferred_element_type=jnp.float32).astype(jnp.bfloat16)
        gate_part, up_part = lax.optimization_barrier((gate_part, up_part))
        gate = gate + gate_part.astype(jnp.float32)
        up = up + up_part.astype(jnp.float32)
    hidden = (jax.nn.silu(gate) * up).astype(jnp.bfloat16)
    return jnp.dot(hidden, down_weight, preferred_element_type=jnp.float32).astype(jnp.bfloat16)
```

```python
import functools

import jax
import jax.numpy as jnp
from jax import lax
from jax.experimental import pallas as pl
from jax.experimental.pallas import tpu as pltpu
from jax.sharding import PartitionSpec as P

ROWS = 64
SLOTS = 4
MESH = pl.DeviceIdType.MESH


def widest(columns, most=1024):
    return max(w for w in range(128, most + 1, 128) if columns % w == 0)


def xor(a, b, size):
    total, bit = 0, 1
    while bit < size:
        total = total + lax.rem(lax.div(a, bit) + lax.div(b, bit), 2) * bit
        bit *= 2
    return total


def kernel(n, peers, tokens, w_gate, w_up, w_down, out, landed, tok, gate_w, up_w, down_w,
           sum_a, sum_b, part_a, part_b, hid_a, hid_b, mine, outgoing,
           load_sem, tok_send, tok_recv, sum_send, sum_recv, credit, hid_send, hid_recv, out_send, out_recv):
    f32, bf16 = jnp.float32, jnp.bfloat16
    m, f = lax.axis_index("mp"), lax.axis_index("ffn")
    pieces, rows, _ = tokens.shape
    chunks = pieces * peers
    half = sum_a.shape[2] // 2
    width = mine.shape[2]
    last = n - 1
    sums, parts, hids = (sum_a, sum_b), (part_a, part_b), (hid_a, hid_b)
    depths = (m, last - m)
    ahead = (m + 1, m - 1)
    behind = (m - 1, m + 1)

    def turn(p):
        return 1 if p == peers - 1 else p + 1

    gate_load = pltpu.make_async_copy(w_gate, gate_w, load_sem.at[0])
    up_load = pltpu.make_async_copy(w_up, up_w, load_sem.at[1])
    down_load = pltpu.make_async_copy(w_down, down_w, load_sem.at[2])
    own_load = pltpu.make_async_copy(tokens, tok.at[pl.ds(0, pieces)], load_sem.at[3])
    own_load.start()
    gate_load.start()
    up_load.start()

    barrier = pltpu.get_barrier_semaphore()
    for p in range(1, peers):
        pl.semaphore_signal(barrier, inc=1, device_id={"ffn": xor(f, turn(p), peers)}, device_id_type=MESH)

    @pl.when(m > 0)
    def _():
        pl.semaphore_signal(barrier, inc=1, device_id={"mp": m - 1}, device_id_type=MESH)

    @pl.when(m < last)
    def _():
        pl.semaphore_signal(barrier, inc=1, device_id={"mp": m + 1}, device_id_type=MESH)

    pl.semaphore_wait(barrier, peers - 1 + jnp.where(m > 0, 1, 0) + jnp.where(m < last, 1, 0))

    def token_copy(p, peer):
        return pltpu.make_async_remote_copy(
            src_ref=tokens, dst_ref=tok.at[pl.ds(p * pieces, pieces)],
            send_sem=tok_send.at[p], recv_sem=tok_recv.at[p],
            device_id={"ffn": peer}, device_id_type=MESH)

    def sum_copy(d, c):
        slot = lax.rem(c, SLOTS)
        return pltpu.make_async_remote_copy(
            src_ref=sums[d].at[slot], dst_ref=sums[d].at[slot],
            send_sem=sum_send.at[d, lax.rem(c, 2)], recv_sem=sum_recv.at[d, slot],
            device_id={"mp": ahead[d]}, device_id_type=MESH)

    def hid_copy(d, c):
        return pltpu.make_async_remote_copy(
            src_ref=hids[d].at[c], dst_ref=hids[d].at[c],
            send_sem=hid_send.at[d, lax.rem(c, 2)], recv_sem=hid_recv.at[d, c],
            device_id={"mp": behind[d]}, device_id_type=MESH)

    def out_copy(c, peer):
        return pltpu.make_async_remote_copy(
            src_ref=outgoing.at[lax.rem(c, 2)], dst_ref=landed.at[c],
            send_sem=out_send.at[lax.rem(c, 2)], recv_sem=out_recv.at[c],
            device_id={"ffn": peer}, device_id_type=MESH)

    for p in range(1, peers):
        token_copy(p, xor(f, turn(p), peers)).start()
    down_load.start()

    def first_matmul(d, c):
        tile = widest(half)

        @pl.when((c >= 0) & (c < chunks))
        def _():
            @pl.loop(0, half // tile)
            def _(j):
                x = tok[c]
                to = pl.multiple_of(j * tile, tile)
                columns = pl.ds(pl.multiple_of(d * half + j * tile, 128), tile)
                parts[d][:, pl.ds(to, tile)] = jnp.dot(
                    x, gate_w[:, columns], preferred_element_type=f32).astype(bf16)
                parts[d][:, pl.ds(pl.multiple_of(half + j * tile, 128), tile)] = jnp.dot(
                    x, up_w[:, columns], preferred_element_type=f32).astype(bf16)

    def first_matmuls(s):
        q = s - jnp.minimum(depths[0], depths[1])

        @pl.when((q >= pieces) & (q < chunks) & (lax.rem(jnp.maximum(q, 0), pieces) == 0))
        def _():
            token_copy(lax.div(q, pieces), f).wait_recv()

        for d in range(2):
            first_matmul(d, s - depths[d])

    def pass_sum(d, s):
        c = s - depths[d]
        depth, slots, part = depths[d], sums[d], parts[d]

        @pl.when((c >= 0) & (c < chunks))
        def _():
            slot = lax.rem(c, SLOTS)

            @pl.when(depth == 0)
            def _():
                slots[slot] = part[...]

            @pl.when(depth > 0)
            def _():
                sum_copy(d, c).wait_recv()

            @pl.when((depth > 0) & (depth < last))
            def _():
                slots[slot] = (slots[slot].astype(f32) + part[...].astype(f32)).astype(bf16)

            @pl.when(depth < last)
            def _():
                @pl.when(c >= SLOTS)
                def _():
                    pl.semaphore_wait(credit.at[d], 1)

                sum_copy(d, c).start()

            @pl.when(depth == last)
            def _():
                gate = slots[slot, :, :half].astype(f32) + part[:, :half].astype(f32)
                up = slots[slot, :, half:].astype(f32) + part[:, half:].astype(f32)
                hids[d][c] = (gate / (1.0 + jnp.exp(-gate)) * up).astype(bf16)
                hid_copy(d, c).start()

                @pl.when(c + SLOTS < chunks)
                def _():
                    pl.semaphore_signal(credit.at[d], inc=1, device_id={"mp": behind[d]}, device_id_type=MESH)

    def pass_hidden(d, s):
        depth = depths[d]
        c = s - (2 * last - depth)

        @pl.when((depth < last) & (c >= 0) & (c < chunks))
        def _():
            hid_copy(d, c).wait_recv()

            @pl.when(depth > 0)
            def _():
                hid_copy(d, c).start()

    def sent(d, s):
        depth = depths[d]
        c = s - depth - 1

        @pl.when((depth < last) & (c >= 0) & (c < chunks))
        def _():
            sum_copy(d, c).wait_send()

            @pl.when((depth > 0) & (c + SLOTS < chunks))
            def _():
                pl.semaphore_signal(credit.at[d], inc=1, device_id={"mp": behind[d]}, device_id_type=MESH)

        h = s - (2 * last - depth) - 1

        @pl.when((depth > 0) & (h >= 0) & (h < chunks))
        def _():
            hid_copy(d, h).wait_send()

    def second_matmul(s):
        c = s - jnp.maximum(2 * last - m, last + m)
        tile = widest(width)

        def product(j):
            columns = pl.ds(pl.multiple_of(j * tile, tile), tile)
            total = jnp.dot(hid_a[c], down_w[pl.ds(0, half), columns], preferred_element_type=f32)
            total += jnp.dot(hid_b[c], down_w[pl.ds(half, half), columns], preferred_element_type=f32)
            return columns, total.astype(bf16)

        @pl.when(c == 0)
        def _():
            down_load.wait()

        @pl.when((c >= 0) & (c < pieces))
        def _():
            @pl.loop(0, width // tile)
            def _(j):
                columns, total = product(j)
                mine[c, :, columns] = total

        @pl.when((c >= pieces) & (c < chunks))
        def _():
            p = lax.div(c, pieces)
            peer = xor(f, jnp.where(p == peers - 1, 1, p + 1), peers)
            par = lax.rem(c, 2)

            @pl.when(c >= pieces + 2)
            def _():
                out_copy(c, peer).wait_send()

            @pl.loop(0, width // tile)
            def _(j):
                columns, total = product(j)
                outgoing[par, :, columns] = total

            out_copy(c, peer).start()

    own_load.wait()
    gate_load.wait()
    up_load.wait()
    first_matmuls(jnp.int32(0))

    @pl.loop(0, chunks + 2 * last)
    def _(s):
        pass_sum(0, s)
        pass_sum(1, s)
        pass_hidden(0, s)
        pass_hidden(1, s)
        sent(0, s)
        sent(1, s)
        first_matmuls(s + 1)
        second_matmul(s)

    for p in range(1, peers):
        token_copy(p, f).wait_send()
    for c in range(pieces, chunks):
        out_copy(c, f).wait_recv()
        pltpu.make_async_copy(landed.at[c], tok.at[c], out_recv.at[c]).start()
    out[...] = mine[...]
    for c in range(pieces, chunks):
        pltpu.make_async_copy(landed.at[c], tok.at[c], out_recv.at[c]).wait()
    for k in range(pieces):
        total = mine[k].astype(f32)
        for p in range(1, peers):
            total += tok[p * pieces + k].astype(f32)
        out[k] = total.astype(bf16)
    for c in range(chunks - min(2, chunks - pieces), chunks):
        out_copy(c, f).wait_send()


def on_device(n, peers, tokens, gate_weight, up_weight, down_weight):
    held, depth = tokens.shape
    hidden, width = down_weight.shape
    rows, half = ROWS, hidden // 2
    pieces = held // rows
    chunks = pieces * peers
    bf16 = jnp.bfloat16
    dma = pltpu.SemaphoreType.DMA
    flops = 6 * chunks * rows * depth * hidden
    out, _ = pl.pallas_call(
        functools.partial(kernel, n, peers),
        out_shape=(jax.ShapeDtypeStruct((pieces, rows, width), bf16),
                   jax.ShapeDtypeStruct((chunks, rows, width), bf16)),
        in_specs=[pl.BlockSpec(memory_space=pl.ANY)] * 4,
        out_specs=(pl.BlockSpec(memory_space=pltpu.VMEM), pl.BlockSpec(memory_space=pl.ANY)),
        scratch_shapes=[
            pltpu.VMEM((chunks, rows, depth), bf16),
            pltpu.VMEM((depth, hidden), bf16),
            pltpu.VMEM((depth, hidden), bf16),
            pltpu.VMEM((hidden, width), bf16),
            pltpu.VMEM((SLOTS, rows, hidden), bf16),
            pltpu.VMEM((SLOTS, rows, hidden), bf16),
            pltpu.VMEM((rows, hidden), bf16),
            pltpu.VMEM((rows, hidden), bf16),
            pltpu.VMEM((chunks, rows, half), bf16),
            pltpu.VMEM((chunks, rows, half), bf16),
            pltpu.VMEM((pieces, rows, width), bf16),
            pltpu.VMEM((2, rows, width), bf16),
            dma((4,)), dma((peers,)), dma((peers,)), dma((2, 2)), dma((2, SLOTS)),
            pltpu.SemaphoreType.REGULAR((2,)), dma((2, 2)), dma((2, chunks)), dma((2,)), dma((chunks,)),
        ],
        compiler_params=pltpu.CompilerParams(
            collective_id=0, has_side_effects=True, vmem_limit_bytes=63 * 1024 * 1024),
        cost_estimate=pl.CostEstimate(
            flops=flops, bytes_accessed=6 * depth * hidden, transcendentals=chunks * rows * half),
    )(tokens.reshape(pieces, rows, depth), gate_weight, up_weight, down_weight)
    return out.reshape(held, width)


def solution(mesh):
    in_specs = (P("ffn", "mp"), P("mp", "ffn"), P("mp", "ffn"), P("ffn", "mp"))
    body = functools.partial(on_device, mesh.shape["mp"], mesh.shape["ffn"])
    return jax.shard_map(body, mesh=mesh, in_specs=in_specs, out_specs=P("ffn", "mp"), check_vma=False)
```

```python
import functools

import jax
import jax.numpy as jnp
from jax import lax
from jax.experimental import pallas as pl
from jax.experimental.pallas import tpu as pltpu
from jax.sharding import PartitionSpec as P

ROWS = 32
GROUP = 2
SLOTS = 8
MESH = pl.DeviceIdType.MESH


def widest(columns, most=1024):
    return max(w for w in range(128, most + 1, 128) if columns % w == 0)


def xor(a, b, size):
    total, bit = 0, 1
    while bit < size:
        total = total + lax.rem(lax.div(a, bit) + lax.div(b, bit), 2) * bit
        bit *= 2
    return total


def kernel(n, peers, tokens, w_gate, w_up, w_down, out, landed, tok, gate_w, up_w, down_w,
           sum_a, sum_b, part_a, part_b, hid_a, hid_b, mine, outgoing,
           load_sem, tok_send, tok_recv, sum_send, sum_recv, credit, hid_send, hid_recv, out_send, out_recv):
    f32, bf16 = jnp.float32, jnp.bfloat16
    m, f = lax.axis_index("mp"), lax.axis_index("ffn")
    pieces = tokens.shape[0]
    blocks = pieces * peers
    chunks = blocks * GROUP
    half = sum_a.shape[2] // 2
    width = mine.shape[2]
    last = n - 1
    sums, parts, hids = (sum_a, sum_b), (part_a, part_b), (hid_a, hid_b)
    depths = (m, last - m)
    ahead = (m + 1, m - 1)
    behind = (m - 1, m + 1)

    def turn(p):
        return 1 if p == peers - 1 else p + 1

    def half_loads(d):
        columns = pl.ds(d * half, half)
        return (pltpu.make_async_copy(w_gate.at[:, columns], gate_w.at[:, columns], load_sem.at[2 * d]),
                pltpu.make_async_copy(w_up.at[:, columns], up_w.at[:, columns], load_sem.at[2 * d + 1]))

    down_load = pltpu.make_async_copy(w_down, down_w, load_sem.at[4])
    own_load = pltpu.make_async_copy(tokens, tok.at[pl.ds(0, pieces)], load_sem.at[5])
    own_load.start()

    @pl.when(depths[0] <= depths[1])
    def _():
        for load in half_loads(0) + half_loads(1):
            load.start()

    @pl.when(depths[0] > depths[1])
    def _():
        for load in half_loads(1) + half_loads(0):
            load.start()

    barrier = pltpu.get_barrier_semaphore()
    for p in range(1, peers):
        pl.semaphore_signal(barrier, inc=1, device_id={"ffn": xor(f, turn(p), peers)}, device_id_type=MESH)

    @pl.when(m > 0)
    def _():
        pl.semaphore_signal(barrier, inc=1, device_id={"mp": m - 1}, device_id_type=MESH)

    @pl.when(m < last)
    def _():
        pl.semaphore_signal(barrier, inc=1, device_id={"mp": m + 1}, device_id_type=MESH)

    pl.semaphore_wait(barrier, peers - 1 + jnp.where(m > 0, 1, 0) + jnp.where(m < last, 1, 0))

    def block_of(c):
        return lax.div(c, GROUP)

    def rows_of(c):
        return pl.ds(pl.multiple_of(lax.rem(c, GROUP) * ROWS, ROWS), ROWS)

    def token_copy(p, peer):
        return pltpu.make_async_remote_copy(
            src_ref=tokens, dst_ref=tok.at[pl.ds(p * pieces, pieces)],
            send_sem=tok_send.at[p], recv_sem=tok_recv.at[p],
            device_id={"ffn": peer}, device_id_type=MESH)

    def sum_copy(d, c):
        slot = lax.rem(c, SLOTS)
        return pltpu.make_async_remote_copy(
            src_ref=sums[d].at[slot], dst_ref=sums[d].at[slot],
            send_sem=sum_send.at[d, lax.rem(c, 2)], recv_sem=sum_recv.at[d, slot],
            device_id={"mp": ahead[d]}, device_id_type=MESH)

    def hid_copy(d, c):
        return pltpu.make_async_remote_copy(
            src_ref=hids[d].at[block_of(c), rows_of(c)], dst_ref=hids[d].at[block_of(c), rows_of(c)],
            send_sem=hid_send.at[d, lax.rem(c, 2)], recv_sem=hid_recv.at[d, c],
            device_id={"mp": behind[d]}, device_id_type=MESH)

    def out_copy(b, peer):
        return pltpu.make_async_remote_copy(
            src_ref=outgoing.at[lax.rem(b, 2)], dst_ref=landed.at[b],
            send_sem=out_send.at[lax.rem(b, 2)], recv_sem=out_recv.at[b],
            device_id={"ffn": peer}, device_id_type=MESH)

    for p in range(1, peers):
        token_copy(p, xor(f, turn(p), peers)).start()
    down_load.start()

    def first_matmul(d, c):
        tile = widest(half)

        @pl.when(c == 0)
        def _():
            for load in half_loads(d):
                load.wait()

        @pl.when((c >= 0) & (c < chunks) & (lax.rem(jnp.maximum(c, 0), GROUP) == 0))
        def _():
            @pl.loop(0, half // tile)
            def _(j):
                x = tok[block_of(c)]
                to = pl.multiple_of(j * tile, tile)
                columns = pl.ds(pl.multiple_of(d * half + j * tile, 128), tile)
                parts[d][:, pl.ds(to, tile)] = jnp.dot(
                    x, gate_w[:, columns], preferred_element_type=f32).astype(bf16)
                parts[d][:, pl.ds(pl.multiple_of(half + j * tile, 128), tile)] = jnp.dot(
                    x, up_w[:, columns], preferred_element_type=f32).astype(bf16)

    def first_matmuls(s):
        q = s - jnp.minimum(depths[0], depths[1])

        held = pieces * GROUP

        @pl.when((q >= held) & (q < chunks) & (lax.rem(jnp.maximum(q, 0), held) == 0))
        def _():
            token_copy(lax.div(q, held), f).wait_recv()

        for d in range(2):
            first_matmul(d, s - depths[d])

    def pass_sum(d, s):
        c = s - depths[d]
        depth, slots, part = depths[d], sums[d], parts[d]

        @pl.when((c >= 0) & (c < chunks))
        def _():
            slot, own = lax.rem(c, SLOTS), rows_of(c)

            @pl.when(depth == 0)
            def _():
                slots[slot] = part[own, :]

            @pl.when(depth > 0)
            def _():
                sum_copy(d, c).wait_recv()

            @pl.when((depth > 0) & (depth < last))
            def _():
                slots[slot] = (slots[slot].astype(f32) + part[own, :].astype(f32)).astype(bf16)

            @pl.when(depth < last)
            def _():
                @pl.when(c >= SLOTS)
                def _():
                    pl.semaphore_wait(credit.at[d], 1)

                sum_copy(d, c).start()

            @pl.when(depth == last)
            def _():
                gate = slots[slot, :, :half].astype(f32) + part[own, :half].astype(f32)
                up = slots[slot, :, half:].astype(f32) + part[own, half:].astype(f32)
                hids[d][block_of(c), own, :] = (gate / (1.0 + jnp.exp(-gate)) * up).astype(bf16)
                hid_copy(d, c).start()

                @pl.when(c + SLOTS < chunks)
                def _():
                    pl.semaphore_signal(credit.at[d], inc=1, device_id={"mp": behind[d]}, device_id_type=MESH)

    def pass_hidden(d, s):
        depth = depths[d]
        c = s - (2 * last - depth)

        @pl.when((depth < last) & (c >= 0) & (c < chunks))
        def _():
            hid_copy(d, c).wait_recv()

            @pl.when(depth > 0)
            def _():
                hid_copy(d, c).start()

    def sent(d, s):
        depth = depths[d]
        c = s - depth - 1

        @pl.when((depth < last) & (c >= 0) & (c < chunks))
        def _():
            sum_copy(d, c).wait_send()

            @pl.when((depth > 0) & (c + SLOTS < chunks))
            def _():
                pl.semaphore_signal(credit.at[d], inc=1, device_id={"mp": behind[d]}, device_id_type=MESH)

        h = s - (2 * last - depth) - 1

        @pl.when((depth > 0) & (h >= 0) & (h < chunks))
        def _():
            hid_copy(d, h).wait_send()

    def second_matmul(s):
        c = s - jnp.maximum(2 * last - m, last + m) - (GROUP - 1)
        b = block_of(jnp.maximum(c, 0))
        part = lax.rem(jnp.maximum(c, 0), GROUP)
        share = width // GROUP
        tile = widest(share)
        ready = (c >= 0) & (c < chunks)

        def product(j):
            columns = pl.ds(pl.multiple_of(part * share + j * tile, tile), tile)
            total = jnp.dot(hid_a[b], down_w[pl.ds(0, half), columns], preferred_element_type=f32)
            total += jnp.dot(hid_b[b], down_w[pl.ds(half, half), columns], preferred_element_type=f32)
            return columns, total.astype(bf16)

        @pl.when(c == 0)
        def _():
            down_load.wait()

        @pl.when(ready & (b < pieces))
        def _():
            @pl.loop(0, share // tile)
            def _(j):
                columns, total = product(j)
                mine[b, :, columns] = total

        @pl.when(ready & (b >= pieces))
        def _():
            p = lax.div(b, pieces)
            peer = xor(f, jnp.where(p == peers - 1, 1, p + 1), peers)
            par = lax.rem(b, 2)

            @pl.when((b >= pieces + 2) & (part == 0))
            def _():
                out_copy(b, peer).wait_send()

            @pl.loop(0, share // tile)
            def _(j):
                columns, total = product(j)
                outgoing[par, :, columns] = total

            @pl.when(part == GROUP - 1)
            def _():
                out_copy(b, peer).start()

    own_load.wait()
    first_matmuls(jnp.int32(0))

    @pl.loop(0, chunks + 2 * last + GROUP - 1)
    def _(s):
        pass_sum(0, s)
        pass_sum(1, s)
        sent(0, s)
        sent(1, s)
        first_matmuls(s + 1)
        pass_hidden(0, s)
        pass_hidden(1, s)
        second_matmul(s)

    for p in range(1, peers):
        token_copy(p, f).wait_send()
    for b in range(pieces, blocks):
        out_copy(b, f).wait_recv()
        pltpu.make_async_copy(landed.at[b], tok.at[b], out_recv.at[b]).start()
    for b in range(pieces, blocks):
        pltpu.make_async_copy(landed.at[b], tok.at[b], out_recv.at[b]).wait()
    for k in range(pieces):
        total = mine[k].astype(f32)
        for p in range(1, peers):
            total += tok[p * pieces + k].astype(f32)
        out[k] = total.astype(bf16)
    for b in range(blocks - min(2, blocks - pieces), blocks):
        out_copy(b, f).wait_send()


def on_device(n, peers, tokens, gate_weight, up_weight, down_weight):
    held, depth = tokens.shape
    hidden, width = down_weight.shape
    rows, half = ROWS * GROUP, hidden // 2
    pieces = held // rows
    blocks = pieces * peers
    chunks = blocks * GROUP
    bf16 = jnp.bfloat16
    dma = pltpu.SemaphoreType.DMA
    flops = 6 * blocks * rows * depth * hidden
    out, _ = pl.pallas_call(
        functools.partial(kernel, n, peers),
        out_shape=(jax.ShapeDtypeStruct((pieces, rows, width), bf16),
                   jax.ShapeDtypeStruct((blocks, rows, width), bf16)),
        in_specs=[pl.BlockSpec(memory_space=pl.ANY)] * 4,
        out_specs=(pl.BlockSpec(memory_space=pltpu.VMEM), pl.BlockSpec(memory_space=pl.ANY)),
        scratch_shapes=[
            pltpu.VMEM((blocks, rows, depth), bf16),
            pltpu.VMEM((depth, hidden), bf16),
            pltpu.VMEM((depth, hidden), bf16),
            pltpu.VMEM((hidden, width), bf16),
            pltpu.VMEM((SLOTS, ROWS, hidden), bf16),
            pltpu.VMEM((SLOTS, ROWS, hidden), bf16),
            pltpu.VMEM((rows, hidden), bf16),
            pltpu.VMEM((rows, hidden), bf16),
            pltpu.VMEM((blocks, rows, half), bf16),
            pltpu.VMEM((blocks, rows, half), bf16),
            pltpu.VMEM((pieces, rows, width), bf16),
            pltpu.VMEM((2, rows, width), bf16),
            dma((6,)), dma((peers,)), dma((peers,)), dma((2, 2)), dma((2, SLOTS)),
            pltpu.SemaphoreType.REGULAR((2,)), dma((2, 2)), dma((2, chunks)), dma((2,)), dma((blocks,)),
        ],
        compiler_params=pltpu.CompilerParams(
            collective_id=0, has_side_effects=True, vmem_limit_bytes=63 * 1024 * 1024),
        cost_estimate=pl.CostEstimate(
            flops=flops, bytes_accessed=6 * depth * hidden, transcendentals=blocks * rows * half),
    )(tokens.reshape(pieces, rows, depth), gate_weight, up_weight, down_weight)
    return out.reshape(held, width)


def solution(mesh):
    in_specs = (P("ffn", "mp"), P("mp", "ffn"), P("mp", "ffn"), P("ffn", "mp"))
    body = functools.partial(on_device, mesh.shape["mp"], mesh.shape["ffn"])
    return jax.shard_map(body, mesh=mesh, in_specs=in_specs, out_specs=P("ffn", "mp"), check_vma=False)
```
